32 devices in a mesh: section: 4 (over x, core), dp: 4 (over z), sp: 2 (over y).
Axes of the slice: x: 2, y: 2, z: 4, core: 2. Of those that a mesh axis runs over, the one named last changes fastest.
Arguments:
- projected: bfloat16 [4, 4, 256, 3, 24, 128], P('section', 'dp', 'sp'), may hold values from -100 to 100, as said below
- seg_ids: int32 [4, 4, 256], P('section', 'dp'), may hold values from 0 to 7, never falling along the last dimension, each value on 1 to 64 neighbouring positions
- condition: bfloat16 [4, 32, 3072], P('section', 'dp'), may hold values from -8 to 8
- w_gate: bfloat16 [4, 3072, 3072], P('section', 'dp'), may hold values from -0.109375 to 0.109375
Outputs:
- handed: bfloat16 [4, 4, 256, 3072], P('section', 'dp', 'sp')
The draws below stay inside these ranges and needn't reach their ends.
Inputs may be any that keep to these rules, and one draw needn't show every extreme that they name: `projected`: Query, key and value entries lie within the range. `seg_ids`: within a row the sample numbers never fall; each of the 8 samples holds 1 to 64 positions and one holds exactly 64.
All inputs are finite; a program needn't handle non-finite values.
Results may differ from the reference program's by a relative error of at most 0.006.
Values may be sent and summed in bfloat16 or wider, within the bound.
A program may use at most 64 MiB of HBM per device.

```python
import math
import jax
import jax.numpy as jnp
import numpy as np
from jax import lax

H = 24
HD = 128
D = 3072
L = 256
SEG = 8
SEGLEN = 64
N_SECTION = 4
N_DP = 4


def draw_projected(key, part):
    first_key = jax.random.fold_in(key, 0)
    shape = (N_SECTION, N_DP, L, 3, H, HD)
    base = jnp.clip(jax.random.normal(first_key, shape, jnp.float32), -4.0, 4.0)
    factor = jnp.array([1.3, 1.3, 1.0], jnp.float32).reshape(1, 1, 1, 3, 1, 1)
    base = base * factor
    query_rows = base[:, :, :, 0]
    key_rows = base[:, :, :, 1]
    values = base[:, :, :, 2]
    stacked = jnp.stack([query_rows, key_rows, values], axis=3)
    return stacked.astype(jnp.bfloat16)


def levels(key, shape, cuts, low, high):
    def one(dim, shards_of):
        steps = jax.random.uniform(jax.random.fold_in(jax.random.fold_in(key, 6), dim), (shards_of,), jnp.float32, low / len(cuts), high / len(cuts))
        return jnp.repeat(jnp.exp(steps), shape[dim] // shards_of).reshape((-1,) + (1,) * (len(shape) - dim - 1))

    gain = one(*cuts[0])
    for cut in cuts[1:]:
        gain = gain * one(*cut)
    return gain


def profile(amount, total, bound, skew):
    loads = [(1 << 20) // math.isqrt(grade ** skew) + 1 for grade in range(2, amount + 1)]
    surplus, counts = total - bound - (amount - 1), [1] * (amount - 1)
    while surplus > 0:
        candidates = [i for i in range(amount - 1) if counts[i] < bound]
        mass, left = sum([loads[i] for i in candidates]), surplus
        for i in candidates:
            addition = min(bound - counts[i], max(1, left * loads[i] // mass), surplus)
            counts[i] = counts[i] + addition
            surplus = surplus - addition
    return np.array([bound] + counts)


def uneven_parts(key, count, total, reach, skew):
    if count == 2:
        one = jax.random.randint(key, (), max(1, total - reach), min(reach, total - 1) + 1)
        return jnp.stack([one, total - one])
    sizes = jnp.asarray(profile(count, total, reach, skew), jnp.int32)
    pairs = (count - 1) // 2
    donor, sink = sizes[1:1 + 2 * pairs:2], sizes[2:2 + 2 * pairs:2]
    slack = jnp.minimum(donor - 1, reach - sink)
    moved = jax.random.randint(jax.random.fold_in(key, 1), (pairs,), 0, 1 << 20) % (slack + 1)
    sizes = sizes.at[1:1 + 2 * pairs:2].set(donor - moved).at[2:2 + 2 * pairs:2].set(sink + moved)
    return sizes[jax.random.permutation(jax.random.fold_in(key, 2), count)]


def bell_draw(stream_key, extent, spread, limit, cuts=(), kind=jnp.bfloat16):
    result = spread * jax.random.normal(stream_key, extent, jnp.float32)
    if cuts:
        result = result * levels(stream_key, extent, cuts, -0.22, 0.18)
    return jnp.clip(result, -limit, limit).astype(kind)


def setup_inputs(seed: int = 0) -> dict:
    seeds = jax.random.split(jax.random.key(seed), 5)
    projected = draw_projected(jax.random.fold_in(seeds[4], 71), 0)
    seg_ids = jax.vmap(lambda own: jnp.searchsorted(jnp.cumsum(uneven_parts(own, SEG, L, SEGLEN, 2)), jnp.arange(L), side="right"))(jax.random.split(seeds[1], N_SECTION * N_DP)).reshape((N_SECTION, N_DP, L)).astype(jnp.int32)
    condition = bell_draw(seeds[2], (N_SECTION, N_DP * SEG, D), 2.0, 8.0, ((0, 4), (1, 4)))
    w_gate = bell_draw(seeds[3], (N_SECTION, D, D), D ** -0.5, 0.109375, ((0, 4), (1, 4)))
    return dict(projected=projected, seg_ids=seg_ids, condition=condition, w_gate=w_gate)


masked_score = -1e+30

def attend_row(exchanged, segment_row):
    query_rows = exchanged[:, 0]
    key_rows = exchanged[:, 1].astype(jnp.float32)
    values = exchanged[:, 2].astype(jnp.float32)
    length = query_rows.shape[0]
    query_block = min(512, length)
    block_count = length // query_block
    scale_factor = 1.0 / math.sqrt(query_rows.shape[2])

    def one_block(block_index):
        first_row = block_index * query_block
        query_part = lax.dynamic_slice_in_dim(query_rows, first_row, query_block, 0).astype(jnp.float32)
        seg_part = lax.dynamic_slice_in_dim(segment_row, first_row, query_block, 0)
        scores = jnp.einsum('qhd,khd->hqk', query_part, key_rows) * scale_factor
        same_segment = seg_part[:, None] == segment_row[None, :]
        scores = jnp.where(same_segment[None], scores, masked_score)
        row_max = lax.optimization_barrier(jnp.max(scores, axis=2, keepdims=True))
        weights = jnp.exp(scores - row_max)
        row_total = lax.optimization_barrier(jnp.sum(weights, axis=2, keepdims=True))
        rounded = weights.astype(jnp.bfloat16)
        mixed_out = jnp.einsum('hqk,khd->qhd', rounded.astype(jnp.float32), values)
        mixed_out = mixed_out / jnp.transpose(row_total, (1, 0, 2))
        return mixed_out.astype(jnp.bfloat16)
    blocks = lax.map(one_block, jnp.arange(block_count, dtype=jnp.int32))
    return blocks.reshape(length, blocks.shape[2], blocks.shape[3])

def reference(projected, seg_ids, condition, w_gate):
    section_outputs = []
    for section_number in range(N_SECTION):
        cond_act = jax.nn.silu(condition[section_number].astype(jnp.float32)).astype(jnp.bfloat16)
        seg_gate = jnp.dot(cond_act, w_gate[section_number], preferred_element_type=jnp.float32)
        seg_gate = seg_gate.reshape(N_DP, SEG, H * HD)

        def one_row(inputs):
            rows, segment_row, gates = inputs
            attended = attend_row(rows, segment_row).reshape(L, H * HD)
            one_hot = (segment_row[:, None] == jnp.arange(SEG, dtype=jnp.int32)[None, :]).astype(jnp.float32)
            token_gate = jnp.dot(one_hot, gates, precision=lax.Precision.HIGHEST)
            return (token_gate * attended.astype(jnp.float32)).astype(jnp.bfloat16)
        section_outputs.append(lax.map(one_row, (projected[section_number], seg_ids[section_number], seg_gate)))
    gated = jnp.stack(section_outputs)
    return jnp.roll(gated, 1, axis=0)
```

```python
import functools
import math

import jax
import jax.numpy as jnp
from jax import lax
from jax.experimental import pallas as pl
from jax.experimental.pallas import tpu as pltpu
from jax.sharding import PartitionSpec as P

masked_score = -1e30
HEADS_PER_CHUNK = 2
CHUNKS_BEFORE_GATE = 4
GATE_TILE = 512
MESH = pl.DeviceIdType.MESH


def relay_kernel(
    sizes,
    x_hbm,
    seg_ref,
    cond_ref,
    w_hbm,
    out_hbm,
    x_vmem,
    w_vmem,
    k_halo,
    v_halo,
    stage,
    act_own,
    act_all,
    partial,
    gate_parts,
    gate_split,
    bias,
    x_sem,
    w_sem,
    k_send,
    k_recv,
    v_send,
    v_recv,
    act_send,
    act_recv,
    part_send,
    part_recv,
    out_send,
    out_recv,
):
    tok, heads, size, length, samples, n_section, n_dp, n_sp, reach = sizes
    width = heads * size
    w_rows = w_vmem.shape[0]
    chunk = HEADS_PER_CHUNK * size
    chunks = heads // HEADS_PER_CHUNK
    section, dp, sp = lax.axis_index("section"), lax.axis_index("dp"), lax.axis_index("sp")
    after = lax.rem(section + 1, n_section)
    before = lax.rem(section + n_section - 1, n_section)

    if n_sp == 1:
        exchanges = []
    elif n_sp == 2:
        exchanges = [(1 - sp, (1 - sp) * (tok - reach), 1 - sp, sp * (tok - reach))]
    else:
        right, left = lax.rem(sp + 1, n_sp), lax.rem(sp + n_sp - 1, n_sp)
        exchanges = [(right, tok - reach, left, tok - reach), (left, 0, right, 0)]
    slots = len(exchanges)

    x_copy = pltpu.make_async_copy(x_hbm, x_vmem, x_sem)
    w_copy = pltpu.make_async_copy(w_hbm.at[0], w_vmem, w_sem)
    x_copy.start()
    w_copy.start()

    barrier = pltpu.get_barrier_semaphore()
    for peer, _, _, _ in exchanges:
        pl.semaphore_signal(barrier, inc=1, device_id=(section, dp, peer), device_id_type=MESH)

    def greet(d, carry):
        pl.semaphore_signal(
            barrier, inc=1, device_id=(section, lax.rem(dp + d, n_dp), sp), device_id_type=MESH
        )
        return carry

    lax.fori_loop(1, n_dp, greet, 0)
    for peer in (after, before):
        pl.semaphore_signal(barrier, inc=1, device_id=(peer, dp, sp), device_id_type=MESH)

    cond = cond_ref[0].astype(jnp.float32)
    act = (cond / (1.0 + jnp.exp(-cond))).astype(jnp.bfloat16).astype(jnp.float32)
    for j in range(n_dp):
        act_own[j] = act[:, j * w_rows : (j + 1) * w_rows]

    pl.semaphore_wait(barrier, slots + n_dp - 1 + 2)

    def act_copy(d):
        peer = lax.rem(dp + d, n_dp)
        return pltpu.make_async_remote_copy(
            src_ref=act_own.at[peer],
            dst_ref=act_all.at[dp],
            send_sem=act_send.at[d],
            recv_sem=act_recv.at[d],
            device_id=(section, peer, sp),
            device_id_type=MESH,
        )

    def halo_copies(slot, c):
        peer, row, _, _ = exchanges[slot]
        rows = pl.ds(row if isinstance(row, int) else pl.multiple_of(row, reach), reach)
        lanes = pl.multiple_of(c * chunk, chunk)
        result = []
        for part, held, send, recv in ((1, k_halo, k_send, k_recv), (2, v_halo, v_send, v_recv)):
            result.append(
                pltpu.make_async_remote_copy(
                    src_ref=x_hbm.at[rows, pl.ds(part * width + lanes, chunk)],
                    dst_ref=held.at[slot, rows, pl.ds(lanes, chunk)],
                    send_sem=send.at[slot, c],
                    recv_sem=recv.at[slot, c],
                    device_id=(section, dp, peer),
                    device_id_type=MESH,
                )
            )
        return result

    def arrived_copies(slot, c):
        _, _, _, row = exchanges[slot]
        rows = pl.ds(row if isinstance(row, int) else pl.multiple_of(row, reach), reach)
        lanes = pl.multiple_of(c * chunk, chunk)
        result = []
        for part, held, send, recv in ((1, k_halo, k_send, k_recv), (2, v_halo, v_send, v_recv)):
            result.append(
                pltpu.make_async_remote_copy(
                    src_ref=x_hbm.at[rows, pl.ds(part * width + lanes, chunk)],
                    dst_ref=held.at[slot, rows, pl.ds(lanes, chunk)],
                    send_sem=send.at[slot, c],
                    recv_sem=recv.at[slot, c],
                    device_id=(section, dp, exchanges[slot][0]),
                    device_id_type=MESH,
                )
            )
        return result

    def part_copy(d):
        peer = lax.rem(dp + d, n_dp)
        return pltpu.make_async_remote_copy(
            src_ref=partial.at[peer],
            dst_ref=gate_parts.at[d],
            send_sem=part_send.at[d],
            recv_sem=part_recv.at[d],
            device_id=(section, peer, sp),
            device_id_type=MESH,
        )

    def out_copy(c):
        lanes = pl.ds(pl.multiple_of(c * chunk, chunk), chunk)
        return pltpu.make_async_remote_copy(
            src_ref=stage.at[:, lanes],
            dst_ref=out_hbm.at[:, lanes],
            send_sem=out_send.at[c],
            recv_sem=out_recv.at[c],
            device_id=(after, dp, sp),
            device_id_type=MESH,
        )

    def start_act(d, carry):
        act_copy(d).start()
        return carry

    lax.fori_loop(1, n_dp, start_act, 0)

    def start_halo(c, carry):
        for slot in range(slots):
            for copy in halo_copies(slot, c):
                copy.start()
        return carry

    lax.fori_loop(0, chunks, start_halo, 0)

    if slots and reach < tok:
        for slot in range(slots):
            row = exchanges[slot][3]
            empty = tok - reach
            first = (reach if row == 0 else 0) if isinstance(row, int) else (1 - sp) * reach
            rows = pl.ds(first if isinstance(first, int) else pl.multiple_of(first, empty), empty)
            k_halo[slot, rows, :] = jnp.zeros((empty, width), jnp.bfloat16)
            v_halo[slot, rows, :] = jnp.zeros((empty, width), jnp.bfloat16)

    def block_segments(index):
        found = jnp.zeros((1, tok), jnp.float32)
        for b in range(n_sp):
            ids = seg_ref[0, :, b * tok : (b + 1) * tok].astype(jnp.float32)
            found = found + jnp.where(index == b, ids, 0.0)
        return found

    own_segments = block_segments(sp)
    query_segments = jnp.transpose(jnp.broadcast_to(own_segments, (tok, tok)))
    for slot in range(slots + 1):
        ids = own_segments if slot == 0 else block_segments(exchanges[slot - 1][2])
        bias[:, slot * tok : (slot + 1) * tok] = jnp.where(
            query_segments == ids, 0.0, masked_score
        )
    which = lax.broadcasted_iota(jnp.int32, (tok, 2 * samples), 1)
    which = jnp.where(which >= samples, which - samples, which).astype(jnp.float32)
    chosen = jnp.where(query_segments[:, : 2 * samples] == which, 1.0, 0.0).astype(jnp.bfloat16)

    act_all[dp] = act_own[dp]

    def wait_act(d, carry):
        act_copy(d).wait_recv()
        return carry

    lax.fori_loop(1, n_dp, wait_act, 0)
    w_copy.wait()
    act_rows = act_all[...].reshape(n_dp * samples, w_rows).astype(jnp.bfloat16)

    def gate_tile(t, carry):
        lanes = pl.ds(pl.multiple_of(t * GATE_TILE, GATE_TILE), GATE_TILE)
        sums = jnp.dot(act_rows, w_vmem[:, lanes], preferred_element_type=jnp.float32)
        partial[:, :, lanes] = sums.reshape(n_dp, samples, GATE_TILE)
        return carry

    lax.fori_loop(0, width // GATE_TILE, gate_tile, 0)

    def start_part(d, carry):
        part_copy(d).start()
        return carry

    lax.fori_loop(1, n_dp, start_part, 0)

    x_copy.wait()
    factor = math.log2(math.e) / math.sqrt(size)
    contract_last = (((1,), (1,)), ((), ()))

    def attend(c):
        for slot in range(slots):
            for copy in arrived_copies(slot, c):
                copy.wait_recv()
        base = pl.multiple_of(c * chunk, chunk)
        for h in range(HEADS_PER_CHUNK):
            lane = base + h * size
            lanes = pl.ds(lane, size)
            query = x_vmem[:, lanes]
            keys = [x_vmem[:, pl.ds(width + lane, size)]]
            values = [x_vmem[:, pl.ds(2 * width + lane, size)]]
            for slot in range(slots):
                keys.append(k_halo[slot, :, lanes])
                values.append(v_halo[slot, :, lanes])
            scores = [
                lax.dot_general(query, key, contract_last, preferred_element_type=jnp.float32)
                + bias[:, i * tok : (i + 1) * tok]
                for i, key in enumerate(keys)
            ]
            top = functools.reduce(jnp.maximum, scores)
            top = jnp.max(top, axis=1, keepdims=True)
            weights = [jnp.exp2((s - top) * factor) for s in scores]
            total = jnp.sum(functools.reduce(jnp.add, weights), axis=1, keepdims=True)
            mixed = sum(
                jnp.dot(w.astype(jnp.bfloat16), v, preferred_element_type=jnp.float32)
                for w, v in zip(weights, values)
            )
            stage[:, lanes] = (mixed / total).astype(jnp.bfloat16)

    def gate_and_send(c):
        lanes = pl.ds(pl.multiple_of(c * chunk, chunk), chunk)
        token_gate = jnp.dot(chosen, gate_split[:, lanes], preferred_element_type=jnp.float32)
        stage[:, lanes] = (token_gate * stage[:, lanes].astype(jnp.float32)).astype(jnp.bfloat16)
        out_copy(c).start()

    def early(c, carry):
        attend(c)
        return carry

    def late(c, carry):
        attend(c)
        gate_and_send(c)
        return carry

    def only_send(c, carry):
        gate_and_send(c)
        return carry

    lax.fori_loop(0, CHUNKS_BEFORE_GATE, early, 0)

    gate_parts[0] = partial[dp]

    def add_part(d, total):
        part_copy(d).wait_recv()
        return total + gate_parts[d]

    gate = lax.fori_loop(1, n_dp, add_part, gate_parts[0])
    high = gate.astype(jnp.bfloat16).astype(jnp.float32)
    gate_split[...] = jnp.concatenate([high, gate - high], axis=0).astype(jnp.bfloat16)

    lax.fori_loop(0, CHUNKS_BEFORE_GATE, only_send, 0)
    lax.fori_loop(CHUNKS_BEFORE_GATE, chunks, late, 0)

    def finish_small(d, carry):
        act_copy(d).wait_send()
        part_copy(d).wait_send()
        return carry

    lax.fori_loop(1, n_dp, finish_small, 0)

    def finish(c, carry):
        for slot in range(slots):
            for copy in halo_copies(slot, c):
                copy.wait_send()
        out_copy(c).wait()
        return carry

    lax.fori_loop(0, chunks, finish, 0)


def shards(projected, seg_ids, condition, w_gate):
    tok, heads, size = projected.shape[2], projected.shape[4], projected.shape[5]
    width = heads * size
    length = seg_ids.shape[2]
    samples, w_rows = condition.shape[1], w_gate.shape[1]
    n_section, n_dp, n_sp = (lax.axis_size(a) for a in ("section", "dp", "sp"))
    reach = min(tok, length // 4)
    slots = 0 if n_sp == 1 else 1 if n_sp == 2 else 2
    chunks = heads // HEADS_PER_CHUNK
    sizes = (tok, heads, size, length, samples, n_section, n_dp, n_sp, reach)
    anywhere = pl.BlockSpec(memory_space=pl.ANY)
    inside = pl.BlockSpec(memory_space=pltpu.VMEM)
    dma = pltpu.SemaphoreType.DMA
    keys = (slots + 1) * tok
    handed = pl.pallas_call(
        functools.partial(relay_kernel, sizes),
        out_shape=jax.ShapeDtypeStruct((tok, width), jnp.bfloat16),
        in_specs=[anywhere, inside, inside, anywhere],
        out_specs=anywhere,
        scratch_shapes=[
            pltpu.VMEM((tok, 3 * width), jnp.bfloat16),
            pltpu.VMEM((w_rows, width), jnp.bfloat16),
            pltpu.VMEM((max(slots, 1), tok, width), jnp.bfloat16),
            pltpu.VMEM((max(slots, 1), tok, width), jnp.bfloat16),
            pltpu.VMEM((tok, width), jnp.bfloat16),
            pltpu.VMEM((n_dp, samples, w_rows), jnp.float32),
            pltpu.VMEM((n_dp, samples, w_rows), jnp.float32),
            pltpu.VMEM((n_dp, samples, width), jnp.float32),
            pltpu.VMEM((n_dp, samples, width), jnp.float32),
            pltpu.VMEM((2 * samples, width), jnp.bfloat16),
            pltpu.VMEM((tok, keys), jnp.float32),
            dma,
            dma,
            dma((max(slots, 1), chunks)),
            dma((max(slots, 1), chunks)),
            dma((max(slots, 1), chunks)),
            dma((max(slots, 1), chunks)),
            dma((n_dp,)),
            dma((n_dp,)),
            dma((n_dp,)),
            dma((n_dp,)),
            dma((chunks,)),
            dma((chunks,)),
        ],
        compiler_params=pltpu.CompilerParams(
            collective_id=0, has_side_effects=True, vmem_limit_bytes=60 * 1024 * 1024
        ),
        cost_estimate=pl.CostEstimate(
            flops=4 * tok * keys * width + 2 * n_dp * samples * w_rows * width,
            bytes_accessed=2 * (3 * tok * width + w_rows * width + tok * width),
            transcendentals=tok * keys * heads,
        ),
    )(projected.reshape(tok, 3 * width), seg_ids, condition, w_gate)
    return handed.reshape(1, 1, tok, width)


def solution(mesh):
    placed = (
        P("section", "dp", "sp", None, None, None),
        P("section", "dp", None),
        P("section", "dp", None),
        P("section", "dp", None),
    )
    return jax.shard_map(
        shards,
        mesh=mesh,
        in_specs=placed,
        out_specs=P("section", "dp", "sp", None),
        check_vma=False,
    )
```

```python
import functools
import math

import jax
import jax.numpy as jnp
from jax import lax
from jax.experimental import pallas as pl
from jax.experimental.pallas import tpu as pltpu
from jax.sharding import PartitionSpec as P

masked_score = -1e30
HEADS_PER_CHUNK = 2
CHUNKS_PER_TILE = 2
TILES_BEFORE_GATE = 1
MESH = pl.DeviceIdType.MESH


def relay_kernel(
    sizes,
    x_hbm,
    seg_ref,
    cond_ref,
    w_hbm,
    out_hbm,
    x_vmem,
    w_vmem,
    k_halo,
    v_halo,
    stage,
    act_own,
    act_all,
    partial,
    gate_parts,
    gate_split,
    bias,
    x_sem,
    w_sem,
    k_send,
    k_recv,
    v_send,
    v_recv,
    act_send,
    act_recv,
    part_send,
    part_recv,
    out_send,
    out_recv,
):
    tok, heads, size, length, samples, n_section, n_dp, n_sp, reach = sizes
    width = heads * size
    w_rows = w_vmem.shape[0]
    chunk = HEADS_PER_CHUNK * size
    chunks = heads // HEADS_PER_CHUNK
    tile = chunk * CHUNKS_PER_TILE
    tiles = chunks // CHUNKS_PER_TILE
    section, dp, sp = lax.axis_index("section"), lax.axis_index("dp"), lax.axis_index("sp")
    after = lax.rem(section + 1, n_section)
    before = lax.rem(section + n_section - 1, n_section)

    if n_sp == 1:
        exchanges = []
    elif n_sp == 2:
        exchanges = [(1 - sp, (1 - sp) * (tok - reach), 1 - sp, sp * (tok - reach))]
    else:
        right, left = lax.rem(sp + 1, n_sp), lax.rem(sp + n_sp - 1, n_sp)
        exchanges = [(right, tok - reach, left, tok - reach), (left, 0, right, 0)]
    slots = len(exchanges)

    x_copy = pltpu.make_async_copy(x_hbm, x_vmem, x_sem)
    w_copy = pltpu.make_async_copy(w_hbm.at[0], w_vmem, w_sem)
    x_copy.start()
    w_copy.start()

    barrier = pltpu.get_barrier_semaphore()
    for peer, _, _, _ in exchanges:
        pl.semaphore_signal(barrier, inc=1, device_id=(section, dp, peer), device_id_type=MESH)

    def greet(d, carry):
        pl.semaphore_signal(
            barrier, inc=1, device_id=(section, lax.rem(dp + d, n_dp), sp), device_id_type=MESH
        )
        return carry

    lax.fori_loop(1, n_dp, greet, 0)
    for peer in (after, before):
        pl.semaphore_signal(barrier, inc=1, device_id=(peer, dp, sp), device_id_type=MESH)

    cond = cond_ref[0].astype(jnp.float32)
    act = (cond / (1.0 + jnp.exp(-cond))).astype(jnp.bfloat16).astype(jnp.float32)
    for j in range(n_dp):
        act_own[j] = act[:, j * w_rows : (j + 1) * w_rows]

    pl.semaphore_wait(barrier, slots + n_dp - 1 + 2)

    def act_copy(d):
        peer = lax.rem(dp + d, n_dp)
        return pltpu.make_async_remote_copy(
            src_ref=act_own.at[peer],
            dst_ref=act_all.at[dp],
            send_sem=act_send.at[d],
            recv_sem=act_recv.at[d],
            device_id=(section, peer, sp),
            device_id_type=MESH,
        )

    def halo_copies(slot, c):
        peer, row, _, _ = exchanges[slot]
        rows = pl.ds(row if isinstance(row, int) else pl.multiple_of(row, reach), reach)
        lanes = pl.multiple_of(c * chunk, chunk)
        result = []
        for part, held, send, recv in ((1, k_halo, k_send, k_recv), (2, v_halo, v_send, v_recv)):
            result.append(
                pltpu.make_async_remote_copy(
                    src_ref=x_hbm.at[rows, pl.ds(part * width + lanes, chunk)],
                    dst_ref=held.at[slot, rows, pl.ds(lanes, chunk)],
                    send_sem=send.at[slot, c],
                    recv_sem=recv.at[slot, c],
                    device_id=(section, dp, peer),
                    device_id_type=MESH,
                )
            )
        return result

    def arrived_copies(slot, c):
        _, _, _, row = exchanges[slot]
        rows = pl.ds(row if isinstance(row, int) else pl.multiple_of(row, reach), reach)
        lanes = pl.multiple_of(c * chunk, chunk)
        result = []
        for part, held, send, recv in ((1, k_halo, k_send, k_recv), (2, v_halo, v_send, v_recv)):
            result.append(
                pltpu.make_async_remote_copy(
                    src_ref=x_hbm.at[rows, pl.ds(part * width + lanes, chunk)],
                    dst_ref=held.at[slot, rows, pl.ds(lanes, chunk)],
                    send_sem=send.at[slot, c],
                    recv_sem=recv.at[slot, c],
                    device_id=(section, dp, exchanges[slot][0]),
                    device_id_type=MESH,
                )
            )
        return result

    def part_copy(t, d):
        peer = lax.rem(dp + d, n_dp)
        lanes = pl.ds(pl.multiple_of(t * tile, tile), tile)
        return pltpu.make_async_remote_copy(
            src_ref=partial.at[peer, :, lanes],
            dst_ref=gate_parts.at[d, :, lanes],
            send_sem=part_send.at[t, d],
            recv_sem=part_recv.at[t, d],
            device_id=(section, peer, sp),
            device_id_type=MESH,
        )

    def out_copy(c):
        lanes = pl.ds(pl.multiple_of(c * chunk, chunk), chunk)
        return pltpu.make_async_remote_copy(
            src_ref=stage.at[:, lanes],
            dst_ref=out_hbm.at[:, lanes],
            send_sem=out_send.at[c],
            recv_sem=out_recv.at[c],
            device_id=(after, dp, sp),
            device_id_type=MESH,
        )

    def start_act(d, carry):
        act_copy(d).start()
        return carry

    lax.fori_loop(1, n_dp, start_act, 0)

    def start_halo(c, carry):
        for slot in range(slots):
            for copy in halo_copies(slot, c):
                copy.start()
        return carry

    lax.fori_loop(0, chunks, start_halo, 0)

    if slots and reach < tok:
        for slot in range(slots):
            row = exchanges[slot][3]
            empty = tok - reach
            first = (reach if row == 0 else 0) if isinstance(row, int) else (1 - sp) * reach
            rows = pl.ds(first if isinstance(first, int) else pl.multiple_of(first, empty), empty)
            k_halo[slot, rows, :] = jnp.zeros((empty, width), jnp.bfloat16)
            v_halo[slot, rows, :] = jnp.zeros((empty, width), jnp.bfloat16)

    def block_segments(index):
        found = jnp.zeros((1, tok), jnp.float32)
        for b in range(n_sp):
            ids = seg_ref[0, :, b * tok : (b + 1) * tok].astype(jnp.float32)
            found = found + jnp.where(index == b, ids, 0.0)
        return found

    own_segments = block_segments(sp)
    query_segments = jnp.transpose(jnp.broadcast_to(own_segments, (tok, tok)))
    for slot in range(slots + 1):
        ids = own_segments if slot == 0 else block_segments(exchanges[slot - 1][2])
        bias[:, slot * tok : (slot + 1) * tok] = jnp.where(
            query_segments == ids, 0.0, masked_score
        )
    which = lax.broadcasted_iota(jnp.int32, (tok, 2 * samples), 1)
    which = jnp.where(which >= samples, which - samples, which).astype(jnp.float32)
    chosen = jnp.where(query_segments[:, : 2 * samples] == which, 1.0, 0.0).astype(jnp.bfloat16)

    act_all[dp] = act_own[dp]

    def wait_act(d, carry):
        act_copy(d).wait_recv()
        return carry

    lax.fori_loop(1, n_dp, wait_act, 0)
    w_copy.wait()
    act_rows = act_all[...].reshape(n_dp * samples, w_rows).astype(jnp.bfloat16)

    def gate_tile(t, carry):
        lanes = pl.ds(pl.multiple_of(t * tile, tile), tile)
        sums = jnp.dot(act_rows, w_vmem[:, lanes], preferred_element_type=jnp.float32)
        partial[:, :, lanes] = sums.reshape(n_dp, samples, tile)

        def start_part(d, carry):
            part_copy(t, d).start()
            return carry

        lax.fori_loop(1, n_dp, start_part, 0)
        return carry

    lax.fori_loop(0, tiles, gate_tile, 0)

    x_copy.wait()
    factor = math.log2(math.e) / math.sqrt(size)
    contract_last = (((1,), (1,)), ((), ()))

    def attend(c):
        for slot in range(slots):
            for copy in arrived_copies(slot, c):
                copy.wait_recv()
        base = pl.multiple_of(c * chunk, chunk)
        for h in range(HEADS_PER_CHUNK):
            lane = base + h * size
            lanes = pl.ds(lane, size)
            query = x_vmem[:, lanes]
            keys = [x_vmem[:, pl.ds(width + lane, size)]]
            values = [x_vmem[:, pl.ds(2 * width + lane, size)]]
            for slot in range(slots):
                keys.append(k_halo[slot, :, lanes])
                values.append(v_halo[slot, :, lanes])
            scores = [
                lax.dot_general(query, key, contract_last, preferred_element_type=jnp.float32)
                + bias[:, i * tok : (i + 1) * tok]
                for i, key in enumerate(keys)
            ]
            top = functools.reduce(jnp.maximum, scores)
            top = jnp.max(top, axis=1, keepdims=True)
            weights = [jnp.exp2((s - top) * factor) for s in scores]
            total = jnp.sum(functools.reduce(jnp.add, weights), axis=1, keepdims=True)
            mixed = sum(
                jnp.dot(w.astype(jnp.bfloat16), v, preferred_element_type=jnp.float32)
                for w, v in zip(weights, values)
            )
            stage[:, lanes] = (mixed / total).astype(jnp.bfloat16)

    def gate_and_send(c):
        lanes = pl.ds(pl.multiple_of(c * chunk, chunk), chunk)
        token_gate = jnp.dot(chosen, gate_split[:, lanes], preferred_element_type=jnp.float32)
        stage[:, lanes] = (token_gate * stage[:, lanes].astype(jnp.float32)).astype(jnp.bfloat16)
        out_copy(c).start()

    def sum_gate(t):
        lanes = pl.ds(pl.multiple_of(t * tile, tile), tile)

        def add_part(d, total):
            part_copy(t, d).wait_recv()
            return total + gate_parts[d, :, lanes]

        gate = lax.fori_loop(1, n_dp, add_part, partial[dp, :, lanes])
        high = gate.astype(jnp.bfloat16).astype(jnp.float32)
        gate_split[:, lanes] = jnp.concatenate([high, gate - high], axis=0).astype(jnp.bfloat16)

    def early(c, carry):
        attend(c)
        return carry

    def only_send(t, carry):
        sum_gate(t)
        for i in range(CHUNKS_PER_TILE):
            gate_and_send(t * CHUNKS_PER_TILE + i)
        return carry

    def late(t, carry):
        sum_gate(t)
        for i in range(CHUNKS_PER_TILE):
            attend(t * CHUNKS_PER_TILE + i)
            gate_and_send(t * CHUNKS_PER_TILE + i)
        return carry

    lax.fori_loop(0, TILES_BEFORE_GATE * CHUNKS_PER_TILE, early, 0)
    lax.fori_loop(0, TILES_BEFORE_GATE, only_send, 0)
    lax.fori_loop(TILES_BEFORE_GATE, tiles, late, 0)

    def finish_small(d, carry):
        act_copy(d).wait_send()

        def finish_part(t, carry):
            part_copy(t, d).wait_send()
            return carry

        lax.fori_loop(0, tiles, finish_part, 0)
        return carry

    lax.fori_loop(1, n_dp, finish_small, 0)

    def finish(c, carry):
        for slot in range(slots):
            for copy in halo_copies(slot, c):
                copy.wait_send()
        out_copy(c).wait()
        return carry

    lax.fori_loop(0, chunks, finish, 0)


def shards(projected, seg_ids, condition, w_gate):
    tok, heads, size = projected.shape[2], projected.shape[4], projected.shape[5]
    width = heads * size
    length = seg_ids.shape[2]
    samples, w_rows = condition.shape[1], w_gate.shape[1]
    n_section, n_dp, n_sp = (lax.axis_size(a) for a in ("section", "dp", "sp"))
    reach = min(tok, length // 4)
    slots = 0 if n_sp == 1 else 1 if n_sp == 2 else 2
    chunks = heads // HEADS_PER_CHUNK
    sizes = (tok, heads, size, length, samples, n_section, n_dp, n_sp, reach)
    anywhere = pl.BlockSpec(memory_space=pl.ANY)
    inside = pl.BlockSpec(memory_space=pltpu.VMEM)
    dma = pltpu.SemaphoreType.DMA
    keys = (slots + 1) * tok
    handed = pl.pallas_call(
        functools.partial(relay_kernel, sizes),
        out_shape=jax.ShapeDtypeStruct((tok, width), jnp.bfloat16),
        in_specs=[anywhere, inside, inside, pl.BlockSpec(memory_space=pltpu.HBM)],
        out_specs=anywhere,
        scratch_shapes=[
            pltpu.VMEM((tok, 3 * width), jnp.bfloat16),
            pltpu.VMEM((w_rows, width), jnp.bfloat16),
            pltpu.VMEM((max(slots, 1), tok, width), jnp.bfloat16),
            pltpu.VMEM((max(slots, 1), tok, width), jnp.bfloat16),
            pltpu.VMEM((tok, width), jnp.bfloat16),
            pltpu.VMEM((n_dp, samples, w_rows), jnp.float32),
            pltpu.VMEM((n_dp, samples, w_rows), jnp.float32),
            pltpu.VMEM((n_dp, samples, width), jnp.float32),
            pltpu.VMEM((n_dp, samples, width), jnp.float32),
            pltpu.VMEM((2 * samples, width), jnp.bfloat16),
            pltpu.VMEM((tok, keys), jnp.float32),
            dma,
            dma,
            dma((max(slots, 1), chunks)),
            dma((max(slots, 1), chunks)),
            dma((max(slots, 1), chunks)),
            dma((max(slots, 1), chunks)),
            dma((n_dp,)),
            dma((n_dp,)),
            dma((chunks // CHUNKS_PER_TILE, n_dp)),
            dma((chunks // CHUNKS_PER_TILE, n_dp)),
            dma((chunks,)),
            dma((chunks,)),
        ],
        compiler_params=pltpu.CompilerParams(
            collective_id=0, has_side_effects=True, vmem_limit_bytes=40 * 1024 * 1024
        ),
        cost_estimate=pl.CostEstimate(
            flops=4 * tok * keys * width + 2 * n_dp * samples * w_rows * width,
            bytes_accessed=2 * (3 * tok * width + w_rows * width + tok * width),
            transcendentals=tok * keys * heads,
        ),
    )(projected.reshape(tok, 3 * width), seg_ids, condition, w_gate)
    return handed.reshape(1, 1, tok, width)


def solution(mesh):
    placed = (
        P("section", "dp", "sp", None, None, None),
        P("section", "dp", None),
        P("section", "dp", None),
        P("section", "dp", None),
    )
    return jax.shard_map(
        shards,
        mesh=mesh,
        in_specs=placed,
        out_specs=P("section", "dp", "sp", None),
        check_vma=False,
    )
```

```python
import functools
import math

import jax
import jax.numpy as jnp
from jax import lax
from jax.experimental import pallas as pl
from jax.experimental.pallas import tpu as pltpu
from jax.sharding import PartitionSpec as P

masked_score = -1e30
HEADS_PER_CHUNK = 2
CHUNKS_PER_TILE = 2
TILES_BEFORE_GATE = 1
MESH = pl.DeviceIdType.MESH


def relay_kernel(
    sizes,
    x_hbm,
    seg_ref,
    cond_ref,
    w_hbm,
    out_hbm,
    x_vmem,
    w_vmem,
    k_halo,
    v_halo,
    stage,
    act_own,
    act_all,
    partial,
    gate_parts,
    gate_split,
    bias,
    x_sem,
    w_sem,
    k_send,
    k_recv,
    v_send,
    v_recv,
    act_send,
    act_recv,
    part_send,
    part_recv,
    out_send,
    out_recv,
):
    tok, heads, size, length, samples, n_section, n_dp, n_sp, reach = sizes
    width = heads * size
    w_rows = w_vmem.shape[0]
    chunk = HEADS_PER_CHUNK * size
    chunks = heads // HEADS_PER_CHUNK
    tile = chunk * CHUNKS_PER_TILE
    tiles = chunks // CHUNKS_PER_TILE
    section, dp, sp = lax.axis_index("section"), lax.axis_index("dp"), lax.axis_index("sp")
    after = lax.rem(section + 1, n_section)
    before = lax.rem(section + n_section - 1, n_section)

    if n_sp == 1:
        exchanges = []
    elif n_sp == 2:
        exchanges = [(1 - sp, (1 - sp) * (tok - reach), 1 - sp, sp * (tok - reach))]
    else:
        right, left = lax.rem(sp + 1, n_sp), lax.rem(sp + n_sp - 1, n_sp)
        exchanges = [(right, tok - reach, left, tok - reach), (left, 0, right, 0)]
    slots = len(exchanges)

    x_copy = pltpu.make_async_copy(x_hbm, x_vmem, x_sem)
    w_copy = pltpu.make_async_copy(w_hbm.at[0], w_vmem, w_sem)
    x_copy.start()
    w_copy.start()

    barrier = pltpu.get_barrier_semaphore()
    for peer, _, _, _ in exchanges:
        pl.semaphore_signal(barrier, inc=1, device_id=(section, dp, peer), device_id_type=MESH)

    def greet(d, carry):
        pl.semaphore_signal(
            barrier, inc=1, device_id=(section, lax.rem(dp + d, n_dp), sp), device_id_type=MESH
        )
        return carry

    lax.fori_loop(1, n_dp, greet, 0)
    for peer in (after, before):
        pl.semaphore_signal(barrier, inc=1, device_id=(peer, dp, sp), device_id_type=MESH)

    cond = cond_ref[0].astype(jnp.float32)
    act = (cond / (1.0 + jnp.exp(-cond))).astype(jnp.bfloat16).astype(jnp.float32)
    for j in range(n_dp):
        act_own[j] = act[:, j * w_rows : (j + 1) * w_rows]

    pl.semaphore_wait(barrier, slots + n_dp - 1 + 2)

    def act_copy(d):
        peer = lax.rem(dp + d, n_dp)
        return pltpu.make_async_remote_copy(
            src_ref=act_own.at[peer],
            dst_ref=act_all.at[dp],
            send_sem=act_send.at[d],
            recv_sem=act_recv.at[d],
            device_id=(section, peer, sp),
            device_id_type=MESH,
        )

    def halo_copies(slot, c):
        peer, row, _, _ = exchanges[slot]
        rows = pl.ds(row if isinstance(row, int) else pl.multiple_of(row, reach), reach)
        lanes = pl.multiple_of(c * chunk, chunk)
        result = []
        for part, held, send, recv in ((1, k_halo, k_send, k_recv), (2, v_halo, v_send, v_recv)):
            result.append(
                pltpu.make_async_remote_copy(
                    src_ref=x_hbm.at[rows, pl.ds(part * width + lanes, chunk)],
                    dst_ref=held.at[slot, rows, pl.ds(lanes, chunk)],
                    send_sem=send.at[slot, c],
                    recv_sem=recv.at[slot, c],
                    device_id=(section, dp, peer),
                    device_id_type=MESH,
                )
            )
        return result

    def arrived_copies(slot, c):
        _, _, _, row = exchanges[slot]
        rows = pl.ds(row if isinstance(row, int) else pl.multiple_of(row, reach), reach)
        lanes = pl.multiple_of(c * chunk, chunk)
        result = []
        for part, held, send, recv in ((1, k_halo, k_send, k_recv), (2, v_halo, v_send, v_recv)):
            result.append(
                pltpu.make_async_remote_copy(
                    src_ref=x_hbm.at[rows, pl.ds(part * width + lanes, chunk)],
                    dst_ref=held.at[slot, rows, pl.ds(lanes, chunk)],
                    send_sem=send.at[slot, c],
                    recv_sem=recv.at[slot, c],
                    device_id=(section, dp, exchanges[slot][0]),
                    device_id_type=MESH,
                )
            )
        return result

    def part_copy(t, d):
        peer = lax.rem(dp + d, n_dp)
        lanes = pl.ds(pl.multiple_of(t * tile, tile), tile)
        return pltpu.make_async_remote_copy(
            src_ref=partial.at[peer, :, lanes],
            dst_ref=gate_parts.at[d, :, lanes],
            send_sem=part_send.at[t, d],
            recv_sem=part_recv.at[t, d],
            device_id=(section, peer, sp),
            device_id_type=MESH,
        )

    def out_copy(c):
        lanes = pl.ds(pl.multiple_of(c * chunk, chunk), chunk)
        return pltpu.make_async_remote_copy(
            src_ref=stage.at[:, lanes],
            dst_ref=out_hbm.at[:, lanes],
            send_sem=out_send.at[c],
            recv_sem=out_recv.at[c],
            device_id=(after, dp, sp),
            device_id_type=MESH,
        )

    def start_act(d, carry):
        act_copy(d).start()
        return carry

    lax.fori_loop(1, n_dp, start_act, 0)

    def start_halo(c, carry):
        for slot in range(slots):
            for copy in halo_copies(slot, c):
                copy.start()
        return carry

    lax.fori_loop(0, chunks, start_halo, 0)

    if slots and reach < tok:
        for slot in range(slots):
            row = exchanges[slot][3]
            empty = tok - reach
            first = (reach if row == 0 else 0) if isinstance(row, int) else (1 - sp) * reach
            rows = pl.ds(first if isinstance(first, int) else pl.multiple_of(first, empty), empty)
            k_halo[slot, rows, :] = jnp.zeros((empty, width), jnp.bfloat16)
            v_halo[slot, rows, :] = jnp.zeros((empty, width), jnp.bfloat16)

    def block_segments(index):
        found = jnp.zeros((1, tok), jnp.float32)
        for b in range(n_sp):
            ids = seg_ref[0, :, b * tok : (b + 1) * tok].astype(jnp.float32)
            found = found + jnp.where(index == b, ids, 0.0)
        return found

    own_segments = block_segments(sp)
    query_segments = jnp.transpose(jnp.broadcast_to(own_segments, (tok, tok)))
    for slot in range(slots + 1):
        ids = own_segments if slot == 0 else block_segments(exchanges[slot - 1][2])
        bias[:, slot * tok : (slot + 1) * tok] = jnp.where(
            query_segments == ids, 0.0, masked_score
        )
    which = lax.broadcasted_iota(jnp.int32, (tok, 2 * samples), 1)
    which = jnp.where(which >= samples, which - samples, which).astype(jnp.float32)
    chosen = jnp.where(query_segments[:, : 2 * samples] == which, 1.0, 0.0).astype(jnp.bfloat16)

    act_all[dp] = act_own[dp]

    def wait_act(d, carry):
        act_copy(d).wait_recv()
        return carry

    lax.fori_loop(1, n_dp, wait_act, 0)
    w_copy.wait()
    act_rows = act_all[...].reshape(n_dp * samples, w_rows).astype(jnp.bfloat16)

    def gate_tile(t, carry):
        lanes = pl.ds(pl.multiple_of(t * tile, tile), tile)
        sums = jnp.dot(act_rows, w_vmem[:, lanes], preferred_element_type=jnp.float32)
        partial[:, :, lanes] = sums.reshape(n_dp, samples, tile)

        def start_part(d, carry):
            part_copy(t, d).start()
            return carry

        lax.fori_loop(1, n_dp, start_part, 0)
        return carry

    lax.fori_loop(0, tiles, gate_tile, 0)

    x_copy.wait()
    factor = math.log2(math.e) / math.sqrt(size)
    contract_last = (((1,), (1,)), ((), ()))

    def attend(c):
        for slot in range(slots):
            for copy in arrived_copies(slot, c):
                copy.wait_recv()
        base = pl.multiple_of(c * chunk, chunk)
        for h in range(HEADS_PER_CHUNK):
            lane = base + h * size
            lanes = pl.ds(lane, size)
            query = x_vmem[:, lanes]
            keys = [x_vmem[:, pl.ds(width + lane, size)]]
            values = [x_vmem[:, pl.ds(2 * width + lane, size)]]
            for slot in range(slots):
                keys.append(k_halo[slot, :, lanes])
                values.append(v_halo[slot, :, lanes])
            scores = [
                lax.dot_general(query, key, contract_last, preferred_element_type=jnp.float32)
                + bias[:, i * tok : (i + 1) * tok]
                for i, key in enumerate(keys)
            ]
            top = functools.reduce(jnp.maximum, scores)
            top = jnp.max(top, axis=1, keepdims=True)
            weights = [jnp.exp2((s - top) * factor) for s in scores]
            total = jnp.sum(functools.reduce(jnp.add, weights), axis=1, keepdims=True)
            mixed = sum(
                jnp.dot(w.astype(jnp.bfloat16), v, preferred_element_type=jnp.float32)
                for w, v in zip(weights, values)
            )
            stage[:, lanes] = (mixed / total).astype(jnp.bfloat16)

    def gate_and_send(c):
        lanes = pl.ds(pl.multiple_of(c * chunk, chunk), chunk)
        token_gate = jnp.dot(chosen, gate_split[:, lanes], preferred_element_type=jnp.float32)
        stage[:, lanes] = (token_gate * stage[:, lanes].astype(jnp.float32)).astype(jnp.bfloat16)
        out_copy(c).start()

    def sum_gate(t):
        lanes = pl.ds(pl.multiple_of(t * tile, tile), tile)

        def add_part(d, total):
            part_copy(t, d).wait_recv()
            return total + gate_parts[d, :, lanes]

        gate = lax.fori_loop(1, n_dp, add_part, partial[dp, :, lanes])
        high = gate.astype(jnp.bfloat16).astype(jnp.float32)
        gate_split[:, lanes] = jnp.concatenate([high, gate - high], axis=0).astype(jnp.bfloat16)

    def early(c, carry):
        attend(c)
        return carry

    def only_send(t, carry):
        sum_gate(t)
        for i in range(CHUNKS_PER_TILE):
            gate_and_send(t * CHUNKS_PER_TILE + i)
        return carry

    def late(t, carry):
        sum_gate(t)
        for i in range(CHUNKS_PER_TILE):
            attend(t * CHUNKS_PER_TILE + i)
            gate_and_send(t * CHUNKS_PER_TILE + i)
        return carry

    lax.fori_loop(0, TILES_BEFORE_GATE * CHUNKS_PER_TILE, early, 0)
    lax.fori_loop(0, TILES_BEFORE_GATE, only_send, 0)
    lax.fori_loop(TILES_BEFORE_GATE, tiles, late, 0)

    def finish_small(d, carry):
        act_copy(d).wait_send()

        def finish_part(t, carry):
            part_copy(t, d).wait_send()
            return carry

        lax.fori_loop(0, tiles, finish_part, 0)
        return carry

    lax.fori_loop(1, n_dp, finish_small, 0)

    def finish(c, carry):
        for slot in range(slots):
            for copy in halo_copies(slot, c):
                copy.wait_send()
        out_copy(c).wait()
        return carry

    lax.fori_loop(0, chunks, finish, 0)


def shards(projected, seg_ids, condition, w_gate):
    tok, heads, size = projected.shape[2], projected.shape[4], projected.shape[5]
    width = heads * size
    length = seg_ids.shape[2]
    samples, w_rows = condition.shape[1], w_gate.shape[1]
    n_section, n_dp, n_sp = (lax.axis_size(a) for a in ("section", "dp", "sp"))
    reach = min(tok, length // 4)
    slots = 0 if n_sp == 1 else 1 if n_sp == 2 else 2
    chunks = heads // HEADS_PER_CHUNK
    sizes = (tok, heads, size, length, samples, n_section, n_dp, n_sp, reach)
    anywhere = pl.BlockSpec(memory_space=pl.ANY)
    inside = pl.BlockSpec(memory_space=pltpu.VMEM)
    dma = pltpu.SemaphoreType.DMA
    keys = (slots + 1) * tok
    handed = pl.pallas_call(
        functools.partial(relay_kernel, sizes),
        out_shape=jax.ShapeDtypeStruct((tok, width), jnp.bfloat16),
        in_specs=[anywhere, inside, inside, pl.BlockSpec(memory_space=pltpu.HBM)],
        out_specs=anywhere,
        scratch_shapes=[
            pltpu.VMEM((tok, 3 * width), jnp.bfloat16),
            pltpu.VMEM((w_rows, width), jnp.bfloat16),
            pltpu.VMEM((max(slots, 1), tok, width), jnp.bfloat16),
            pltpu.VMEM((max(slots, 1), tok, width), jnp.bfloat16),
            pltpu.VMEM((tok, width), jnp.bfloat16),
            pltpu.VMEM((n_dp, samples, w_rows), jnp.float32),
            pltpu.VMEM((n_dp, samples, w_rows), jnp.float32),
            pltpu.VMEM((n_dp, samples, width), jnp.float32),
            pltpu.VMEM((n_dp, samples, width), jnp.float32),
            pltpu.VMEM((2 * samples, width), jnp.bfloat16),
            pltpu.VMEM((tok, keys), jnp.float32),
            dma,
            dma,
            dma((max(slots, 1), chunks)),
            dma((max(slots, 1), chunks)),
            dma((max(slots, 1), chunks)),
            dma((max(slots, 1), chunks)),
            dma((n_dp,)),
            dma((n_dp,)),
            dma((chunks // CHUNKS_PER_TILE, n_dp)),
            dma((chunks // CHUNKS_PER_TILE, n_dp)),
            dma((chunks,)),
            dma((chunks,)),
        ],
        compiler_params=pltpu.CompilerParams(
            collective_id=0, has_side_effects=True, vmem_limit_bytes=49 * 1024 * 1024
        ),
        cost_estimate=pl.CostEstimate(
            flops=4 * tok * keys * width + 2 * n_dp * samples * w_rows * width,
            bytes_accessed=2 * (3 * tok * width + w_rows * width + tok * width),
            transcendentals=tok * keys * heads,
        ),
    )(projected.reshape(tok, 3 * width), seg_ids, condition, w_gate)
    return handed.reshape(1, 1, tok, width)


def solution(mesh):
    placed = (
        P("section", "dp", "sp", None, None, None),
        P("section", "dp", None),
        P("section", "dp", None),
        P("section", "dp", None),
    )
    return jax.shard_map(
        shards,
        mesh=mesh,
        in_specs=placed,
        out_specs=P("section", "dp", "sp", None),
        check_vma=False,
    )
```

```python
import functools
import math

import jax
import jax.numpy as jnp
from jax import lax
from jax.experimental import pallas as pl
from jax.experimental.pallas import tpu as pltpu
from jax.sharding import PartitionSpec as P

masked_score = -1e30
HEADS_PER_CHUNK = 2
CHUNKS_PER_TILE = 2
TILES_BEFORE_GATE = 1
MESH = pl.DeviceIdType.MESH


def relay_kernel(
    sizes,
    x_ref,
    seg_ref,
    cond_ref,
    w_hbm,
    out_hbm,
    w_vmem,
    k_halo,
    v_halo,
    stage,
    act_own,
    act_all,
    partial,
    gate_parts,
    gate_split,
    bias,
    w_sem,
    k_send,
    k_recv,
    v_send,
    v_recv,
    act_send,
    act_recv,
    part_send,
    part_recv,
    out_send,
    out_recv,
):
    tok, heads, size, length, samples, n_section, n_dp, n_sp, reach = sizes
    width = heads * size
    w_rows = w_vmem.shape[0]
    chunk = HEADS_PER_CHUNK * size
    chunks = heads // HEADS_PER_CHUNK
    tile = chunk * CHUNKS_PER_TILE
    tiles = chunks // CHUNKS_PER_TILE
    section, dp, sp = lax.axis_index("section"), lax.axis_index("dp"), lax.axis_index("sp")
    after = lax.rem(section + 1, n_section)
    before = lax.rem(section + n_section - 1, n_section)

    if n_sp == 1:
        exchanges = []
    elif n_sp == 2:
        exchanges = [(1 - sp, (1 - sp) * (tok - reach), 1 - sp, sp * (tok - reach))]
    else:
        right, left = lax.rem(sp + 1, n_sp), lax.rem(sp + n_sp - 1, n_sp)
        exchanges = [(right, tok - reach, left, tok - reach), (left, 0, right, 0)]
    slots = len(exchanges)

    w_copy = pltpu.make_async_copy(w_hbm.at[0], w_vmem, w_sem)
    w_copy.start()

    barrier = pltpu.get_barrier_semaphore()
    for peer, _, _, _ in exchanges:
        pl.semaphore_signal(barrier, inc=1, device_id=(section, dp, peer), device_id_type=MESH)

    def greet(d, carry):
        pl.semaphore_signal(
            barrier, inc=1, device_id=(section, lax.rem(dp + d, n_dp), sp), device_id_type=MESH
        )
        return carry

    lax.fori_loop(1, n_dp, greet, 0)
    for peer in (after, before):
        pl.semaphore_signal(barrier, inc=1, device_id=(peer, dp, sp), device_id_type=MESH)

    cond = cond_ref[0].astype(jnp.float32)
    act = (cond / (1.0 + jnp.exp(-cond))).astype(jnp.bfloat16).astype(jnp.float32)
    for j in range(n_dp):
        act_own[j] = act[:, j * w_rows : (j + 1) * w_rows]

    pl.semaphore_wait(barrier, slots + n_dp - 1 + 2)

    def act_copy(d):
        peer = lax.rem(dp + d, n_dp)
        return pltpu.make_async_remote_copy(
            src_ref=act_own.at[peer],
            dst_ref=act_all.at[dp],
            send_sem=act_send.at[d],
            recv_sem=act_recv.at[d],
            device_id=(section, peer, sp),
            device_id_type=MESH,
        )

    def halo_copies(slot, c):
        peer, row, _, _ = exchanges[slot]
        rows = pl.ds(row if isinstance(row, int) else pl.multiple_of(row, reach), reach)
        lanes = pl.multiple_of(c * chunk, chunk)
        result = []
        for part, held, send, recv in ((1, k_halo, k_send, k_recv), (2, v_halo, v_send, v_recv)):
            result.append(
                pltpu.make_async_remote_copy(
                    src_ref=x_ref.at[rows, pl.ds(part * width + lanes, chunk)],
                    dst_ref=held.at[slot, rows, pl.ds(lanes, chunk)],
                    send_sem=send.at[slot, c],
                    recv_sem=recv.at[slot, c],
                    device_id=(section, dp, peer),
                    device_id_type=MESH,
                )
            )
        return result

    def arrived_copies(slot, c):
        _, _, _, row = exchanges[slot]
        rows = pl.ds(row if isinstance(row, int) else pl.multiple_of(row, reach), reach)
        lanes = pl.multiple_of(c * chunk, chunk)
        result = []
        for part, held, send, recv in ((1, k_halo, k_send, k_recv), (2, v_halo, v_send, v_recv)):
            result.append(
                pltpu.make_async_remote_copy(
                    src_ref=x_ref.at[rows, pl.ds(part * width + lanes, chunk)],
                    dst_ref=held.at[slot, rows, pl.ds(lanes, chunk)],
                    send_sem=send.at[slot, c],
                    recv_sem=recv.at[slot, c],
                    device_id=(section, dp, exchanges[slot][0]),
                    device_id_type=MESH,
                )
            )
        return result

    def part_copy(t, d):
        peer = lax.rem(dp + d, n_dp)
        lanes = pl.ds(pl.multiple_of(t * tile, tile), tile)
        return pltpu.make_async_remote_copy(
            src_ref=partial.at[peer, :, lanes],
            dst_ref=gate_parts.at[d, :, lanes],
            send_sem=part_send.at[t, d],
            recv_sem=part_recv.at[t, d],
            device_id=(section, peer, sp),
            device_id_type=MESH,
        )

    def out_copy(c):
        lanes = pl.ds(pl.multiple_of(c * chunk, chunk), chunk)
        return pltpu.make_async_remote_copy(
            src_ref=stage.at[:, lanes],
            dst_ref=out_hbm.at[:, lanes],
            send_sem=out_send.at[c],
            recv_sem=out_recv.at[c],
            device_id=(after, dp, sp),
            device_id_type=MESH,
        )

    def start_act(d, carry):
        act_copy(d).start()
        return carry

    lax.fori_loop(1, n_dp, start_act, 0)

    def start_halo(c, carry):
        for slot in range(slots):
            for copy in halo_copies(slot, c):
                copy.start()
        return carry

    lax.fori_loop(0, chunks, start_halo, 0)

    if slots and reach < tok:
        for slot in range(slots):
            row = exchanges[slot][3]
            empty = tok - reach
            first = (reach if row == 0 else 0) if isinstance(row, int) else (1 - sp) * reach
            rows = pl.ds(first if isinstance(first, int) else pl.multiple_of(first, empty), empty)
            k_halo[slot, rows, :] = jnp.zeros((empty, width), jnp.bfloat16)
            v_halo[slot, rows, :] = jnp.zeros((empty, width), jnp.bfloat16)

    def block_segments(index):
        found = jnp.zeros((1, tok), jnp.float32)
        for b in range(n_sp):
            ids = seg_ref[0, :, b * tok : (b + 1) * tok].astype(jnp.float32)
            found = found + jnp.where(index == b, ids, 0.0)
        return found

    own_segments = block_segments(sp)
    query_segments = jnp.transpose(jnp.broadcast_to(own_segments, (tok, tok)))
    for slot in range(slots + 1):
        ids = own_segments if slot == 0 else block_segments(exchanges[slot - 1][2])
        bias[:, slot * tok : (slot + 1) * tok] = jnp.where(
            query_segments == ids, 0.0, masked_score
        )
    which = lax.broadcasted_iota(jnp.int32, (tok, 2 * samples), 1)
    which = jnp.where(which >= samples, which - samples, which).astype(jnp.float32)
    chosen = jnp.where(query_segments[:, : 2 * samples] == which, 1.0, 0.0).astype(jnp.bfloat16)

    act_all[dp] = act_own[dp]

    def wait_act(d, carry):
        act_copy(d).wait_recv()
        return carry

    lax.fori_loop(1, n_dp, wait_act, 0)
    w_copy.wait()
    act_rows = act_all[...].reshape(n_dp * samples, w_rows).astype(jnp.bfloat16)

    def gate_tile(t, carry):
        lanes = pl.ds(pl.multiple_of(t * tile, tile), tile)
        sums = jnp.dot(act_rows, w_vmem[:, lanes], preferred_element_type=jnp.float32)
        partial[:, :, lanes] = sums.reshape(n_dp, samples, tile)

        def start_part(d, carry):
            part_copy(t, d).start()
            return carry

        lax.fori_loop(1, n_dp, start_part, 0)
        return carry

    lax.fori_loop(0, tiles, gate_tile, 0)

    factor = math.log2(math.e) / math.sqrt(size)
    contract_last = (((1,), (1,)), ((), ()))

    def attend(c):
        for slot in range(slots):
            for copy in arrived_copies(slot, c):
                copy.wait_recv()
        base = pl.multiple_of(c * chunk, chunk)
        for h in range(HEADS_PER_CHUNK):
            lane = base + h * size
            lanes = pl.ds(lane, size)
            query = x_ref[:, lanes]
            keys = [x_ref[:, pl.ds(width + lane, size)]]
            values = [x_ref[:, pl.ds(2 * width + lane, size)]]
            for slot in range(slots):
                keys.append(k_halo[slot, :, lanes])
                values.append(v_halo[slot, :, lanes])
            scores = [
                lax.dot_general(query, key, contract_last, preferred_element_type=jnp.float32)
                + bias[:, i * tok : (i + 1) * tok]
                for i, key in enumerate(keys)
            ]
            top = functools.reduce(jnp.maximum, scores)
            top = jnp.max(top, axis=1, keepdims=True)
            weights = [jnp.exp2((s - top) * factor) for s in scores]
            total = jnp.sum(functools.reduce(jnp.add, weights), axis=1, keepdims=True)
            mixed = sum(
                jnp.dot(w.astype(jnp.bfloat16), v, preferred_element_type=jnp.float32)
                for w, v in zip(weights, values)
            )
            stage[:, lanes] = (mixed / total).astype(jnp.bfloat16)

    def gate_and_send(c):
        lanes = pl.ds(pl.multiple_of(c * chunk, chunk), chunk)
        token_gate = jnp.dot(chosen, gate_split[:, lanes], preferred_element_type=jnp.float32)
        stage[:, lanes] = (token_gate * stage[:, lanes].astype(jnp.float32)).astype(jnp.bfloat16)
        out_copy(c).start()

    def sum_gate(t):
        lanes = pl.ds(pl.multiple_of(t * tile, tile), tile)

        def add_part(d, total):
            part_copy(t, d).wait_recv()
            return total + gate_parts[d, :, lanes]

        gate = lax.fori_loop(1, n_dp, add_part, partial[dp, :, lanes])
        high = gate.astype(jnp.bfloat16).astype(jnp.float32)
        gate_split[:, lanes] = jnp.concatenate([high, gate - high], axis=0).astype(jnp.bfloat16)

    def early(c, carry):
        attend(c)
        return carry

    def only_send(t, carry):
        sum_gate(t)
        for i in range(CHUNKS_PER_TILE):
            gate_and_send(t * CHUNKS_PER_TILE + i)
        return carry

    def late(t, carry):
        sum_gate(t)
        for i in range(CHUNKS_PER_TILE):
            attend(t * CHUNKS_PER_TILE + i)
            gate_and_send(t * CHUNKS_PER_TILE + i)
        return carry

    lax.fori_loop(0, TILES_BEFORE_GATE * CHUNKS_PER_TILE, early, 0)
    lax.fori_loop(0, TILES_BEFORE_GATE, only_send, 0)
    lax.fori_loop(TILES_BEFORE_GATE, tiles, late, 0)

    def finish_small(d, carry):
        act_copy(d).wait_send()

        def finish_part(t, carry):
            part_copy(t, d).wait_send()
            return carry

        lax.fori_loop(0, tiles, finish_part, 0)
        return carry

    lax.fori_loop(1, n_dp, finish_small, 0)

    def finish(c, carry):
        for slot in range(slots):
            for copy in halo_copies(slot, c):
                copy.wait_send()
        out_copy(c).wait()
        return carry

    lax.fori_loop(0, chunks, finish, 0)


def shards(projected, seg_ids, condition, w_gate):
    tok, heads, size = projected.shape[2], projected.shape[4], projected.shape[5]
    width = heads * size
    length = seg_ids.shape[2]
    samples, w_rows = condition.shape[1], w_gate.shape[1]
    n_section, n_dp, n_sp = (lax.axis_size(a) for a in ("section", "dp", "sp"))
    reach = min(tok, length // 4)
    slots = 0 if n_sp == 1 else 1 if n_sp == 2 else 2
    chunks = heads // HEADS_PER_CHUNK
    sizes = (tok, heads, size, length, samples, n_section, n_dp, n_sp, reach)
    anywhere = pl.BlockSpec(memory_space=pl.ANY)
    inside = pl.BlockSpec(memory_space=pltpu.VMEM)
    dma = pltpu.SemaphoreType.DMA
    keys = (slots + 1) * tok
    handed = pl.pallas_call(
        functools.partial(relay_kernel, sizes),
        out_shape=jax.ShapeDtypeStruct((tok, width), jnp.bfloat16),
        in_specs=[inside, inside, inside, pl.BlockSpec(memory_space=pltpu.HBM)],
        out_specs=anywhere,
        scratch_shapes=[
            pltpu.VMEM((w_rows, width), jnp.bfloat16),
            pltpu.VMEM((max(slots, 1), tok, width), jnp.bfloat16),
            pltpu.VMEM((max(slots, 1), tok, width), jnp.bfloat16),
            pltpu.VMEM((tok, width), jnp.bfloat16),
            pltpu.VMEM((n_dp, samples, w_rows), jnp.float32),
            pltpu.VMEM((n_dp, samples, w_rows), jnp.float32),
            pltpu.VMEM((n_dp, samples, width), jnp.float32),
            pltpu.VMEM((n_dp, samples, width), jnp.float32),
            pltpu.VMEM((2 * samples, width), jnp.bfloat16),
            pltpu.VMEM((tok, keys), jnp.float32),
            dma,
            dma((max(slots, 1), chunks)),
            dma((max(slots, 1), chunks)),
            dma((max(slots, 1), chunks)),
            dma((max(slots, 1), chunks)),
            dma((n_dp,)),
            dma((n_dp,)),
            dma((chunks // CHUNKS_PER_TILE, n_dp)),
            dma((chunks // CHUNKS_PER_TILE, n_dp)),
            dma((chunks,)),
            dma((chunks,)),
        ],
        compiler_params=pltpu.CompilerParams(
            collective_id=0, has_side_effects=True, vmem_limit_bytes=49 * 1024 * 1024
        ),
        cost_estimate=pl.CostEstimate(
            flops=4 * tok * keys * width + 2 * n_dp * samples * w_rows * width,
            bytes_accessed=2 * (3 * tok * width + w_rows * width + tok * width),
            transcendentals=tok * keys * heads,
        ),
    )(projected.reshape(tok, 3 * width), seg_ids, condition, w_gate)
    return handed.reshape(1, 1, tok, width)


def solution(mesh):
    placed = (
        P("section", "dp", "sp", None, None, None),
        P("section", "dp", None),
        P("section", "dp", None),
        P("section", "dp", None),
    )
    return jax.shard_map(
        shards,
        mesh=mesh,
        in_specs=placed,
        out_specs=P("section", "dp", "sp", None),
        check_vma=False,
    )
```

```python
import functools
import math

import jax
import jax.numpy as jnp
from jax import lax
from jax.experimental import pallas as pl
from jax.experimental.pallas import tpu as pltpu
from jax.sharding import PartitionSpec as P

masked_score = -1e30
HEADS_PER_CHUNK = 2
CHUNKS_PER_TILE = 2
TILES_BEFORE_GATE = 1
MESH = pl.DeviceIdType.MESH


def relay_kernel(
    sizes,
    x_ref,
    seg_ref,
    cond_ref,
    w_hbm,
    out_hbm,
    w_vmem,
    k_halo,
    v_halo,
    stage,
    act_own,
    act_all,
    partial,
    gate_parts,
    gate_split,
    bias,
    w_sem,
    k_send,
    k_recv,
    v_send,
    v_recv,
    act_send,
    act_recv,
    part_send,
    part_recv,
    out_send,
    out_recv,
):
    tok, heads, size, length, samples, n_section, n_dp, n_sp, reach = sizes
    width = heads * size
    w_rows = w_vmem.shape[0]
    chunk = HEADS_PER_CHUNK * size
    chunks = heads // HEADS_PER_CHUNK
    tile = chunk * CHUNKS_PER_TILE
    tiles = chunks // CHUNKS_PER_TILE
    section, dp, sp = lax.axis_index("section"), lax.axis_index("dp"), lax.axis_index("sp")
    after = lax.rem(section + 1, n_section)
    before = lax.rem(section + n_section - 1, n_section)

    if n_sp == 1:
        exchanges = []
    elif n_sp == 2:
        exchanges = [(1 - sp, (1 - sp) * (tok - reach), 1 - sp, sp * (tok - reach))]
    else:
        right, left = lax.rem(sp + 1, n_sp), lax.rem(sp + n_sp - 1, n_sp)
        exchanges = [(right, tok - reach, left, tok - reach), (left, 0, right, 0)]
    slots = len(exchanges)

    w_copy = pltpu.make_async_copy(w_hbm.at[0], w_vmem, w_sem)
    w_copy.start()

    barrier = pltpu.get_barrier_semaphore()
    for peer, _, _, _ in exchanges:
        pl.semaphore_signal(barrier, inc=1, device_id=(section, dp, peer), device_id_type=MESH)

    def greet(d, carry):
        pl.semaphore_signal(
            barrier, inc=1, device_id=(section, lax.rem(dp + d, n_dp), sp), device_id_type=MESH
        )
        return carry

    lax.fori_loop(1, n_dp, greet, 0)
    for peer in (after, before):
        pl.semaphore_signal(barrier, inc=1, device_id=(peer, dp, sp), device_id_type=MESH)

    cond = cond_ref[0].astype(jnp.float32)
    act = (cond / (1.0 + jnp.exp(-cond))).astype(jnp.bfloat16).astype(jnp.float32)
    for j in range(n_dp):
        act_own[j] = act[:, j * w_rows : (j + 1) * w_rows]

    pl.semaphore_wait(barrier, slots + n_dp - 1 + 2)

    def act_copy(d):
        peer = lax.rem(dp + d, n_dp)
        return pltpu.make_async_remote_copy(
            src_ref=act_own.at[peer],
            dst_ref=act_all.at[dp],
            send_sem=act_send.at[d],
            recv_sem=act_recv.at[d],
            device_id=(section, peer, sp),
            device_id_type=MESH,
        )

    def halo_copies(slot, c):
        peer, row, _, _ = exchanges[slot]
        rows = pl.ds(row if isinstance(row, int) else pl.multiple_of(row, reach), reach)
        lanes = pl.multiple_of(c * chunk, chunk)
        result = []
        for part, held, send, recv in ((1, k_halo, k_send, k_recv), (2, v_halo, v_send, v_recv)):
            result.append(
                pltpu.make_async_remote_copy(
                    src_ref=x_ref.at[rows, pl.ds(part * width + lanes, chunk)],
                    dst_ref=held.at[slot, rows, pl.ds(lanes, chunk)],
                    send_sem=send.at[slot, c],
                    recv_sem=recv.at[slot, c],
                    device_id=(section, dp, peer),
                    device_id_type=MESH,
                )
            )
        return result

    def arrived_copies(slot, c):
        _, _, _, row = exchanges[slot]
        rows = pl.ds(row if isinstance(row, int) else pl.multiple_of(row, reach), reach)
        lanes = pl.multiple_of(c * chunk, chunk)
        result = []
        for part, held, send, recv in ((1, k_halo, k_send, k_recv), (2, v_halo, v_send, v_recv)):
            result.append(
                pltpu.make_async_remote_copy(
                    src_ref=x_ref.at[rows, pl.ds(part * width + lanes, chunk)],
                    dst_ref=held.at[slot, rows, pl.ds(lanes, chunk)],
                    send_sem=send.at[slot, c],
                    recv_sem=recv.at[slot, c],
                    device_id=(section, dp, exchanges[slot][0]),
                    device_id_type=MESH,
                )
            )
        return result

    def part_copy(t, d):
        peer = lax.rem(dp + d, n_dp)
        lanes = pl.ds(pl.multiple_of(t * tile, tile), tile)
        return pltpu.make_async_remote_copy(
            src_ref=partial.at[peer, :, lanes],
            dst_ref=gate_parts.at[d, :, lanes],
            send_sem=part_send.at[t, d],
            recv_sem=part_recv.at[t, d],
            device_id=(section, peer, sp),
            device_id_type=MESH,
        )

    def out_copy(c):
        lanes = pl.ds(pl.multiple_of(c * chunk, chunk), chunk)
        return pltpu.make_async_remote_copy(
            src_ref=stage.at[:, lanes],
            dst_ref=out_hbm.at[:, lanes],
            send_sem=out_send.at[c],
            recv_sem=out_recv.at[c],
            device_id=(after, dp, sp),
            device_id_type=MESH,
        )

    def start_act(d, carry):
        act_copy(d).start()
        return carry

    def start_halo(c, carry):
        for slot in range(slots):
            for copy in halo_copies(slot, c):
                copy.start()
        return carry

    lax.fori_loop(0, 1, start_halo, 0)
    lax.fori_loop(1, n_dp, start_act, 0)
    lax.fori_loop(1, chunks, start_halo, 0)

    if slots and reach < tok:
        for slot in range(slots):
            row = exchanges[slot][3]
            empty = tok - reach
            first = (reach if row == 0 else 0) if isinstance(row, int) else (1 - sp) * reach
            rows = pl.ds(first if isinstance(first, int) else pl.multiple_of(first, empty), empty)
            k_halo[slot, rows, :] = jnp.zeros((empty, width), jnp.bfloat16)
            v_halo[slot, rows, :] = jnp.zeros((empty, width), jnp.bfloat16)

    def block_segments(index):
        found = jnp.zeros((1, tok), jnp.float32)
        for b in range(n_sp):
            ids = seg_ref[0, :, b * tok : (b + 1) * tok].astype(jnp.float32)
            found = found + jnp.where(index == b, ids, 0.0)
        return found

    own_segments = block_segments(sp)
    query_segments = jnp.transpose(jnp.broadcast_to(own_segments, (tok, tok)))
    for slot in range(slots + 1):
        ids = own_segments if slot == 0 else block_segments(exchanges[slot - 1][2])
        bias[:, slot * tok : (slot + 1) * tok] = jnp.where(
            query_segments == ids, 0.0, masked_score
        )
    which = lax.broadcasted_iota(jnp.int32, (tok, 2 * samples), 1)
    which = jnp.where(which >= samples, which - samples, which).astype(jnp.float32)
    chosen = jnp.where(query_segments[:, : 2 * samples] == which, 1.0, 0.0).astype(jnp.bfloat16)

    act_all[dp] = act_own[dp]

    def wait_act(d, carry):
        act_copy(d).wait_recv()
        return carry

    lax.fori_loop(1, n_dp, wait_act, 0)
    w_copy.wait()
    act_rows = act_all[...].reshape(n_dp * samples, w_rows).astype(jnp.bfloat16)

    def gate_tile(t, carry):
        lanes = pl.ds(pl.multiple_of(t * tile, tile), tile)
        sums = jnp.dot(act_rows, w_vmem[:, lanes], preferred_element_type=jnp.float32)
        partial[:, :, lanes] = sums.reshape(n_dp, samples, tile)

        def start_part(d, carry):
            part_copy(t, d).start()
            return carry

        lax.fori_loop(1, n_dp, start_part, 0)
        return carry

    lax.fori_loop(0, tiles, gate_tile, 0)

    factor = math.log2(math.e) / math.sqrt(size)
    contract_last = (((1,), (1,)), ((), ()))

    def attend(c):
        for slot in range(slots):
            for copy in arrived_copies(slot, c):
                copy.wait_recv()
        base = pl.multiple_of(c * chunk, chunk)
        for h in range(HEADS_PER_CHUNK):
            lane = base + h * size
            lanes = pl.ds(lane, size)
            query = x_ref[:, lanes]
            keys = [x_ref[:, pl.ds(width + lane, size)]]
            values = [x_ref[:, pl.ds(2 * width + lane, size)]]
            for slot in range(slots):
                keys.append(k_halo[slot, :, lanes])
                values.append(v_halo[slot, :, lanes])
            scores = [
                lax.dot_general(query, key, contract_last, preferred_element_type=jnp.float32)
                + bias[:, i * tok : (i + 1) * tok]
                for i, key in enumerate(keys)
            ]
            top = functools.reduce(jnp.maximum, scores)
            top = jnp.max(top, axis=1, keepdims=True)
            weights = [jnp.exp2((s - top) * factor) for s in scores]
            total = jnp.sum(functools.reduce(jnp.add, weights), axis=1, keepdims=True)
            mixed = sum(
                jnp.dot(w.astype(jnp.bfloat16), v, preferred_element_type=jnp.float32)
                for w, v in zip(weights, values)
            )
            stage[:, lanes] = (mixed / total).astype(jnp.bfloat16)

    def gate_and_send(c):
        lanes = pl.ds(pl.multiple_of(c * chunk, chunk), chunk)
        token_gate = jnp.dot(chosen, gate_split[:, lanes], preferred_element_type=jnp.float32)
        stage[:, lanes] = (token_gate * stage[:, lanes].astype(jnp.float32)).astype(jnp.bfloat16)
        out_copy(c).start()

    def sum_gate(t):
        lanes = pl.ds(pl.multiple_of(t * tile, tile), tile)

        def add_part(d, total):
            part_copy(t, d).wait_recv()
            return total + gate_parts[d, :, lanes]

        gate = lax.fori_loop(1, n_dp, add_part, partial[dp, :, lanes])
        high = gate.astype(jnp.bfloat16).astype(jnp.float32)
        gate_split[:, lanes] = jnp.concatenate([high, gate - high], axis=0).astype(jnp.bfloat16)

    def early(c, carry):
        attend(c)
        return carry

    def only_send(t, carry):
        sum_gate(t)
        for i in range(CHUNKS_PER_TILE):
            gate_and_send(t * CHUNKS_PER_TILE + i)
        return carry

    def late(t, carry):
        sum_gate(t)
        for i in range(CHUNKS_PER_TILE):
            attend(t * CHUNKS_PER_TILE + i)
            gate_and_send(t * CHUNKS_PER_TILE + i)
        return carry

    lax.fori_loop(0, TILES_BEFORE_GATE * CHUNKS_PER_TILE, early, 0)
    lax.fori_loop(0, TILES_BEFORE_GATE, only_send, 0)
    lax.fori_loop(TILES_BEFORE_GATE, tiles, late, 0)

    def finish_small(d, carry):
        act_copy(d).wait_send()

        def finish_part(t, carry):
            part_copy(t, d).wait_send()
            return carry

        lax.fori_loop(0, tiles, finish_part, 0)
        return carry

    lax.fori_loop(1, n_dp, finish_small, 0)

    def finish(c, carry):
        for slot in range(slots):
            for copy in halo_copies(slot, c):
                copy.wait_send()
        out_copy(c).wait()
        return carry

    lax.fori_loop(0, chunks, finish, 0)


def shards(projected, seg_ids, condition, w_gate):
    tok, heads, size = projected.shape[2], projected.shape[4], projected.shape[5]
    width = heads * size
    length = seg_ids.shape[2]
    samples, w_rows = condition.shape[1], w_gate.shape[1]
    n_section, n_dp, n_sp = (lax.axis_size(a) for a in ("section", "dp", "sp"))
    reach = min(tok, length // 4)
    slots = 0 if n_sp == 1 else 1 if n_sp == 2 else 2
    chunks = heads // HEADS_PER_CHUNK
    sizes = (tok, heads, size, length, samples, n_section, n_dp, n_sp, reach)
    anywhere = pl.BlockSpec(memory_space=pl.ANY)
    inside = pl.BlockSpec(memory_space=pltpu.VMEM)
    dma = pltpu.SemaphoreType.DMA
    keys = (slots + 1) * tok
    handed = pl.pallas_call(
        functools.partial(relay_kernel, sizes),
        out_shape=jax.ShapeDtypeStruct((tok, width), jnp.bfloat16),
        in_specs=[inside, inside, inside, pl.BlockSpec(memory_space=pltpu.HBM)],
        out_specs=anywhere,
        scratch_shapes=[
            pltpu.VMEM((w_rows, width), jnp.bfloat16),
            pltpu.VMEM((max(slots, 1), tok, width), jnp.bfloat16),
            pltpu.VMEM((max(slots, 1), tok, width), jnp.bfloat16),
            pltpu.VMEM((tok, width), jnp.bfloat16),
            pltpu.VMEM((n_dp, samples, w_rows), jnp.float32),
            pltpu.VMEM((n_dp, samples, w_rows), jnp.float32),
            pltpu.VMEM((n_dp, samples, width), jnp.float32),
            pltpu.VMEM((n_dp, samples, width), jnp.float32),
            pltpu.VMEM((2 * samples, width), jnp.bfloat16),
            pltpu.VMEM((tok, keys), jnp.float32),
            dma,
            dma((max(slots, 1), chunks)),
            dma((max(slots, 1), chunks)),
            dma((max(slots, 1), chunks)),
            dma((max(slots, 1), chunks)),
            dma((n_dp,)),
            dma((n_dp,)),
            dma((chunks // CHUNKS_PER_TILE, n_dp)),
            dma((chunks // CHUNKS_PER_TILE, n_dp)),
            dma((chunks,)),
            dma((chunks,)),
        ],
        compiler_params=pltpu.CompilerParams(
            collective_id=0, has_side_effects=True, vmem_limit_bytes=49 * 1024 * 1024
        ),
        cost_estimate=pl.CostEstimate(
            flops=4 * tok * keys * width + 2 * n_dp * samples * w_rows * width,
            bytes_accessed=2 * (3 * tok * width + w_rows * width + tok * width),
            transcendentals=tok * keys * heads,
        ),
    )(projected.reshape(tok, 3 * width), seg_ids, condition, w_gate)
    return handed.reshape(1, 1, tok, width)


def solution(mesh):
    placed = (
        P("section", "dp", "sp", None, None, None),
        P("section", "dp", None),
        P("section", "dp", None),
        P("section", "dp", None),
    )
    return jax.shard_map(
        shards,
        mesh=mesh,
        in_specs=placed,
        out_specs=P("section", "dp", "sp", None),
        check_vma=False,
    )
```
